32 devices in a mesh: groups: 2 (over y), row: 16 (over z, x, core).
Axes of the slice: x: 2, y: 2, z: 4, core: 2. Of those that a mesh axis runs over, the one named last changes fastest.
Arguments:
- p_tiles: bfloat16 [128, 64, 1024], P(('groups', 'row')), parts along dimension 0, may hold values from -0.59765625 to 0.59765625
- p_cols: int32 [128, 16], P(('groups', 'row')), parts along dimension 0, may hold values from 0 to 63, as said below
- p_count: int32 [128], P(('groups', 'row')), parts along dimension 0, may hold values from 8 to 16, as said below
- m_tiles: bfloat16 [128, 64, 1024], P(('groups', 'row')), parts along dimension 0, may hold values from -0.75 to 0.75
- m_cols: int32 [128, 16], P(('groups', 'row')), parts along dimension 0, may hold values from 0 to 63, as said below
- m_count: int32 [128], P(('groups', 'row')), parts along dimension 0, may hold values from 8 to 16, as said below
- g_tiles: bfloat16 [128, 3, 64, 1024], P(('groups', 'row')), parts along dimension 0, may hold values from -0.023925781 to 0.023925781
- basis_atom: int32 [8192], P('groups'), parts along dimension 0, may hold values from 0 to 639, never falling along the last dimension, each value on 1 to 12 neighbouring positions
- atom_slot: int32 [1280], P('groups'), parts along dimension 0, may hold values from 0 to 639, each once
Outputs:
- w_tiles: float32 [128, 64, 1024], P(('groups', 'row')), parts along dimension 0
- forces: float32 [3, 1280], P(None, ('groups', 'row')), parts along dimension 1
The draws below stay inside these ranges and needn't reach their ends.
There are 2 independent parts, one for each index of `groups`. The reference program is written for one: setup_inputs(seed, part) draws one part's arguments, and reference() takes and returns one part's arrays. A program takes and returns all parts, laid end to end along the dimension named above; each array names one. Nothing has to cross between parts.
Inputs may be any that keep to these rules, and one draw needn't show every extreme that they name: `p_cols`: each tile row n lists 16 different tile columns, each within 8 of n counted around the cycle of 64 tile columns. `m_cols`: each tile row n lists 16 different tile columns, each within 8 of n counted around the cycle of 64 tile columns. `p_count`: the live slots of a tile row come first; some tile row has all 16 live in every draw. `m_count`: the live slots of a tile row come first; some tile row has all 16 live in every draw.
All inputs are finite; a program needn't handle non-finite values.
Results may differ from the reference program's by a relative error of at most 0.005.
Values may be sent and summed in bfloat16 or wider, within the bound.
A program may use at most 128 MiB of HBM per device.

```python
import math
import jax
import jax.numpy as jnp
import numpy as np
from jax import lax

GS = 64
BAND = 8
CAP = 16
NB = 64
ORDER = 4096
ATOMS = 640


def column_lists(key):
    row_keys = jax.random.split(key, NB)
    orders = jax.vmap(lambda row_key: jax.random.permutation(row_key, 2 * BAND + 1))(row_keys)
    offsets = orders[:, :CAP].astype(jnp.int32) - BAND
    return ((jnp.arange(NB, dtype=jnp.int32)[:, None] + offsets) % NB).astype(jnp.int32)


def slot_counts(key):
    counts = jax.random.randint(key, (NB,), CAP // 2, CAP + 1, dtype=jnp.int32)
    fullest = jax.random.randint(jax.random.fold_in(key, 7), (), 0, NB, dtype=jnp.int32)
    return counts.at[fullest].set(CAP)


def draw_p_cols(key, part):
    key = jax.random.fold_in(key, 101)
    return column_lists(key)


def draw_m_cols(key, part):
    key = jax.random.fold_in(key, 202)
    return column_lists(key)


def draw_p_count(key, part):
    key = jax.random.fold_in(key, 303)
    return slot_counts(key)


def draw_m_count(key, part):
    key = jax.random.fold_in(key, 404)
    return slot_counts(key)


def shard_levels(key, extent, cuts, low, largest):
    factor_of = 1.0
    for position, parts in cuts:
        steps = jax.random.uniform(jax.random.fold_in(jax.random.fold_in(key, 6), position), (parts,), jnp.float32, low / len(cuts), largest / len(cuts))
        factor_of = factor_of * jnp.repeat(jnp.exp(steps), extent[position] // parts).reshape((-1,) + (1,) * (len(extent) - 1 - position))
    return factor_of


def split_up(amount, total, reach, lean):
    weights = [(1 << 20) // math.isqrt(grade ** lean) + 1 for grade in range(2, amount + 1)]
    rest, given = total - reach - (amount - 1), [1] * (amount - 1)
    while rest > 0:
        movable = [i for i in range(amount - 1) if given[i] < reach]
        pool, budget = sum([weights[i] for i in movable]), rest
        for i in movable:
            addition = min(reach - given[i], max(1, budget * weights[i] // pool), rest)
            given[i] = given[i] + addition
            rest = rest - addition
    return np.array([reach] + given)


def ragged_sizes(key, number_of, total, limit, slope):
    if number_of == 2:
        one = jax.random.randint(key, (), max(1, total - limit), min(limit, total - 1) + 1)
        return jnp.stack([one, total - one])
    lengths = jnp.asarray(split_up(number_of, total, limit, slope), jnp.int32)
    couples = (number_of - 1) // 2
    source_of, sink = lengths[1:1 + 2 * couples:2], lengths[2:2 + 2 * couples:2]
    room = jnp.minimum(source_of - 1, limit - sink)
    moved = jax.random.randint(jax.random.fold_in(key, 1), (couples,), 0, 1 << 20) % (room + 1)
    lengths = lengths.at[1:1 + 2 * couples:2].set(source_of - moved).at[2:2 + 2 * couples:2].set(sink + moved)
    return lengths[jax.random.permutation(jax.random.fold_in(key, 2), number_of)]


def scatter_about(own_key, dims, width, limit, cuts=(), held_as=jnp.bfloat16):
    level = shard_levels(own_key, dims, cuts, -0.22, 0.18) if cuts else 1.0
    array = jax.random.normal(own_key, dims, jnp.float32) * width * level
    return jnp.minimum(jnp.maximum(array, -limit), limit).astype(held_as)


def setup_inputs(seed: int = 0, part: int = 0) -> dict:
    seeds = jax.random.split(jax.random.key(seed), 10)
    own_keys = jax.random.split(jax.random.fold_in(seeds[9], part), 10)
    return {
        "p_tiles": scatter_about(own_keys[0], (NB, GS, CAP * GS), 0.1, 0.59765625, ((0, 16),)),
        "p_cols": draw_p_cols(jax.random.fold_in(jax.random.fold_in(seeds[9], part), 71), part),
        "p_count": draw_p_count(jax.random.fold_in(jax.random.fold_in(seeds[9], part), 71), part),
        "m_tiles": scatter_about(own_keys[3], (NB, GS, CAP * GS), GS ** -0.5, 0.75, ((0, 16),)),
        "m_cols": draw_m_cols(jax.random.fold_in(jax.random.fold_in(seeds[9], part), 71), part),
        "m_count": draw_m_count(jax.random.fold_in(jax.random.fold_in(seeds[9], part), 71), part),
        "g_tiles": scatter_about(own_keys[6], (NB, 3, GS, CAP * GS), 0.004, 0.023925781, ((0, 16),)),
        "basis_atom": jnp.searchsorted(jnp.cumsum(ragged_sizes(own_keys[7], ATOMS, ORDER, 2 * ORDER // ATOMS, 0)), jnp.arange(ORDER), side="right").astype(jnp.int32),
        "atom_slot": jax.random.permutation(own_keys[8], ATOMS).astype(jnp.int32),
    }


def live_grid(packed, counts):
    tile_grid = packed.reshape(NB, GS, CAP, GS)
    is_live = jnp.arange(CAP, dtype=jnp.int32)[None, :] < counts[:, None]
    return jnp.where(is_live[:, None, :, None], tile_grid, jnp.zeros((), tile_grid.dtype))


def band_form(packed, cols, counts):
    band_width = 2 * BAND + 1
    tile_grid = packed.reshape(NB, GS, CAP, GS).astype(jnp.float32)
    offset_index = (cols - jnp.arange(NB, dtype=jnp.int32)[:, None] + BAND) % NB
    is_live = jnp.arange(CAP, dtype=jnp.int32)[None, :] < counts[:, None]
    selector = (offset_index[:, :, None] == jnp.arange(band_width, dtype=jnp.int32)[None, None, :]) & is_live[:, :, None]
    return jnp.einsum("kasb,ksf->kafb", tile_grid, selector.astype(jnp.float32))


def reference(p_tiles, p_cols, p_count, m_tiles, m_cols, m_count, g_tiles, basis_atom, atom_slot):
    band_span = 2 * BAND + 1
    p_grid = live_grid(p_tiles, p_count).astype(jnp.float32)
    m_band = band_form(m_tiles, m_cols, m_count)
    p_band = band_form(p_tiles, p_cols, p_count)
    is_live = jnp.arange(CAP, dtype=jnp.int32)[None, :] < p_count[:, None]
    span_index = jnp.arange(band_span, dtype=jnp.int32)

    def one_row(tile_row):
        offsets = (p_cols[tile_row] - tile_row + BAND) % NB - BAND
        m_rows = m_band[(tile_row + offsets) % NB]
        m_wide = jnp.pad(m_rows, ((0, 0), (0, 0), (2 * BAND, 2 * BAND), (0, 0)))
        m_pieces = jax.vmap(lambda member, start: lax.dynamic_slice_in_dim(member, start, 4 * BAND + 1, 1))(m_wide, BAND - offsets)
        x_row = jnp.einsum("asb,sboc->aoc", p_grid[tile_row], m_pieces)
        x_round = lax.optimization_barrier(x_row.astype(jnp.bfloat16)).astype(jnp.float32)
        x_pieces = jax.vmap(lambda start: lax.dynamic_slice_in_dim(x_round, start, band_span, 1))(offsets + BAND)
        source_rows = (tile_row + offsets[:, None] + span_index[None, :] - BAND) % NB
        p_pieces = p_band[source_rows, :, (2 * BAND - span_index)[None, :], :]
        w_row = jnp.einsum("saub,subc->asc", x_pieces, p_pieces)
        return jnp.where(is_live[tile_row][None, :, None], w_row, 0.0)

    w_grid = lax.map(one_row, jnp.arange(NB, dtype=jnp.int32))
    w_tiles = w_grid.reshape(NB, GS, CAP * GS)
    g_grid = g_tiles.reshape(NB, 3, GS, CAP, GS).astype(jnp.float32)
    row_sums = jnp.einsum("kcasb,kasb->kca", g_grid, w_grid)
    col_sums = jnp.einsum("kcasb,kasb->kcsb", g_grid, w_grid)
    col_basis = (p_cols[:, :, None] * GS + jnp.arange(GS, dtype=jnp.int32)[None, None, :]).reshape(-1)
    col_atoms = basis_atom[col_basis]
    per_atom = jnp.zeros((3, ATOMS), jnp.float32)
    per_atom = per_atom.at[:, basis_atom].add(row_sums.transpose(1, 0, 2).reshape(3, -1))
    per_atom = per_atom.at[:, col_atoms].add(-col_sums.transpose(1, 0, 2, 3).reshape(3, -1))
    forces = jnp.zeros((3, ATOMS), jnp.float32).at[:, atom_slot].set(-2.0 * per_atom)
    return w_tiles, forces
```

```python
import functools
import jax
import jax.numpy as jnp
from jax import lax
from jax.experimental import pallas as pl
from jax.experimental.pallas import tpu as pltpu
from jax.sharding import PartitionSpec as P

BAND = 8
L = 128
F32 = jnp.float32
BF = jnp.bfloat16
MESH = pl.DeviceIdType.MESH


def kernel(n, inv_p, inv_m, idx_w, p_ref, m_ref, g_ref, cid_ref, w_ref, f_ref,
           pt, mt, gt, pfull, gfull, mbuf, pbuf, xacc, xb, wacc, wt, onehot,
           ms, mr, ps, pr):
    me = lax.axis_index("row")
    core = lax.rem(me, 2)
    sibling = me + 1 - 2 * core

    def at(shift):
        return lax.rem(me + shift + n, n)

    up1, dn1, up2, dn2 = at(2), at(-2), at(4), at(-4)
    barrier = pltpu.get_barrier_semaphore()
    for peer in (sibling, up1, dn1, up2, dn2):
        pl.semaphore_signal(barrier, inc=1, device_id={"row": peer}, device_id_type=MESH)

    def rows(at_super, count=2):
        return pl.ds(pl.multiple_of(at_super * L, L), count * L)

    def split(src, r, dst):
        for p in range(8):
            v = src[:, p * L:(p + 1) * L]
            dst[2 * p, r * 64:(r + 1) * 64, :] = v[:, :64]
            dst[2 * p + 1, r * 64:(r + 1) * 64, :] = v[:, 64:]
        dst[16, r * 64:(r + 1) * 64, :] = jnp.zeros((64, 64), BF)

    def pick(src, inv, r, u):
        a = src[inv[r, 2 * u], r * 64:(r + 1) * 64, :]
        b = src[inv[r, 2 * u + 1], r * 64:(r + 1) * 64, :]
        return jnp.concatenate([a, b], axis=1)

    for r in range(4):
        split(m_ref.at[r], r, mt)
        sup = r // 2
        for u in range(sup, sup + 9):
            mbuf[pl.ds(pl.multiple_of((4 + 2 * core) * L, L) + r * 64, 64),
                 (u - sup) * L:(u - sup + 1) * L] = pick(mt, inv_m, r, u)
    pl.semaphore_wait(barrier, 5)

    def copy(buf, src_at, dst_at, col, width, sends, recvs, i, peer):
        cols = pl.ds(col, width * L)
        return pltpu.make_async_remote_copy(
            src_ref=buf.at[rows(src_at), cols], dst_ref=buf.at[rows(dst_at), cols],
            send_sem=sends.at[i], recv_sem=recvs.at[i],
            device_id={"row": peer}, device_id_type=MESH)

    own_m = 4 + 2 * core
    m_up = copy(mbuf, own_m, 2 * core, 0, 9, ms, mr, 0, up1)
    m_dn = copy(mbuf, own_m, 8 + 2 * core, 0, 9, ms, mr, 1, dn1)
    m_sib = copy(mbuf, own_m, own_m, 0, 9, ms, mr, 2, sibling)
    f_at = 8 - 6 * core
    m_fwd = copy(mbuf, f_at, f_at, 0, 9, ms, mr, 3, sibling)
    m_up.start()
    m_dn.start()
    m_sib.start()

    own_p = 8 + 2 * core
    for r in range(4):
        split(p_ref.at[r], r, pt)
        sup = r // 2
        for u in range(10):
            if sup <= u < sup + 9:
                v = pick(pt, inv_p, r, u)
                pfull[r * 64:(r + 1) * 64, u * L:(u + 1) * L] = v
                pbuf[pl.ds(pl.multiple_of(own_p * L, L) + r * 64, 64),
                     (u - sup) * L:(u - sup + 1) * L] = v
            else:
                pfull[r * 64:(r + 1) * 64, u * L:(u + 1) * L] = jnp.zeros((64, L), BF)
    p_up = copy(pbuf, own_p, 4 + 2 * core, L, 8, ps, pr, 0, up1)
    p_dn = copy(pbuf, own_p, 12 + 2 * core, 0, 8, ps, pr, 1, dn1)
    p_up2 = copy(pbuf, own_p, 2 * core, 5 * L, 4, ps, pr, 2, up2)
    p_dn2 = copy(pbuf, own_p, 16 + 2 * core, 0, 4, ps, pr, 3, dn2)
    p_sib = copy(pbuf, own_p, own_p, 0, 9, ps, pr, 4, sibling)
    p_fwd_a = copy(pbuf, 4 + 2 * core, 4 + 2 * core, L, 8, ps, pr, 5, sibling)
    p_fwd_b = copy(pbuf, 12 + 2 * core, 12 + 2 * core, 0, 8, ps, pr, 6, sibling)
    far_at = 16 - 14 * core
    p_fwd_c = copy(pbuf, far_at, far_at, pl.multiple_of(core * 5 * L, L), 4, ps, pr, 7, sibling)
    for c in (p_up, p_dn, p_up2, p_dn2, p_sib):
        c.start()

    for c in range(3):
        for r in range(4):
            split(g_ref.at[r, c], r, gt)
            for u in range(10):
                gfull[c, r * 64:(r + 1) * 64, u * L:(u + 1) * L] = pick(gt, inv_p, r, u)
    slots = onehot.shape[1]
    for s in range(slots // L):
        ids = lax.broadcasted_iota(jnp.int32, (10 * L, L), 1) + s * L
        onehot[:, s * L:(s + 1) * L] = jnp.where(cid_ref[...] == ids, 1.0, 0.0).astype(BF)

    xacc[...] = jnp.zeros(xacc.shape, F32)
    wacc[...] = jnp.zeros(wacc.shape, F32)

    def add_x(j):
        xacc[:, j * L:(j + 9) * L] += jnp.dot(
            pfull[:, j * L:(j + 1) * L], mbuf[rows(j + 2 * core, 1), :],
            preferred_element_type=F32)

    def add_w(k):
        q0, q1 = max(0, 8 - k), min(8, 17 - k)
        m0 = k + q0 - 8
        width = q1 - q0 + 1
        wacc[:, m0 * L:(m0 + width) * L] += jnp.dot(
            xb[:, k * L:(k + 1) * L],
            pbuf[rows(k + 2 * core, 1), q0 * L:(q1 + 1) * L],
            preferred_element_type=F32)

    add_x(4)
    add_x(5)
    m_up.wait_recv()
    m_dn.wait_recv()
    m_fwd.start()
    for j in (0, 1, 8, 9):
        add_x(j)
    m_sib.wait_recv()
    m_fwd.wait_recv()
    for j in (2, 3, 6, 7):
        add_x(j)
    xb[...] = xacc[...].astype(BF)
    add_w(8)
    add_w(9)
    p_up.wait_recv()
    p_fwd_a.start()
    p_dn.wait_recv()
    p_fwd_b.start()
    for k in (4, 5, 12, 13):
        add_w(k)
    p_up2.wait_recv()
    p_dn2.wait_recv()
    p_fwd_c.start()
    for k in (0, 1, 16, 17):
        add_w(k)
    p_sib.wait_recv()
    p_fwd_a.wait_recv()
    p_fwd_b.wait_recv()
    for k in (6, 7, 10, 11):
        add_w(k)
    p_fwd_c.wait_recv()
    for k in (2, 3, 14, 15):
        add_w(k)

    lane = lax.broadcasted_iota(jnp.int32, (4 * 64, L), 1)
    by_row = jnp.zeros((4 * 64, L), F32)
    sub = lax.broadcasted_iota(jnp.int32, (8, 10 * L), 0)
    by_col = jnp.zeros((8, 10 * L), F32)
    for c in range(3):
        prod = wacc[...] * gfull[c].astype(F32)
        by_row = jnp.where(lane == c, jnp.sum(prod, axis=1, keepdims=True), by_row)
        by_col = jnp.where(sub == c, jnp.sum(prod, axis=0, keepdims=True), by_col)
    net_rows = jnp.transpose(by_row)[:8]
    net = jnp.concatenate(
        [-by_col[:, :4 * L], net_rows - by_col[:, 4 * L:6 * L], -by_col[:, 6 * L:]], axis=1)
    high = net.astype(BF).astype(F32)
    rest = net - high
    mid = rest.astype(BF).astype(F32)
    low = rest - mid
    parts = jnp.concatenate([high, mid, low, jnp.zeros_like(low)], axis=0).astype(BF)
    summed = jnp.dot(parts, onehot[...], preferred_element_type=F32)
    f_ref[...] = -2.0 * (summed[0:8] + summed[8:16] + summed[16:24])

    for t in range(20):
        wt[t] = wacc[:, t * 64:(t + 1) * 64]
    wt[20] = jnp.zeros((4 * 64, 64), F32)
    for r in range(4):
        for p in range(8):
            a = wt[idx_w[r, 2 * p], r * 64:(r + 1) * 64, :]
            b = wt[idx_w[r, 2 * p + 1], r * 64:(r + 1) * 64, :]
            w_ref[r, :, p * L:(p + 1) * L] = jnp.concatenate([a, b], axis=1)

    for c in (m_up, m_dn, m_sib, m_fwd, p_up, p_dn, p_up2, p_dn2, p_sib,
              p_fwd_a, p_fwd_b, p_fwd_c):
        c.wait_send()


def slot_maps(cols, counts, first_row, cycle):
    tile_rows, slot_count = cols.shape
    local = jnp.arange(tile_rows, dtype=jnp.int32)[:, None]
    place = (cols - (first_row + local) + BAND) % cycle + local
    live = jnp.arange(slot_count, dtype=jnp.int32)[None, :] < counts[:, None]
    width = tile_rows + 2 * BAND
    hit = (place[:, :, None] == jnp.arange(width, dtype=jnp.int32)) & live[:, :, None]
    slot = jnp.arange(slot_count, dtype=jnp.int32)[None, :, None]
    inverse = slot_count + jnp.sum(jnp.where(hit, slot - slot_count, 0), axis=1)
    return inverse, jnp.where(live, place, width)


def body(p_tiles, p_cols, p_count, m_tiles, m_cols, m_count, g_tiles, basis_atom, atom_slot):
    n = lax.axis_size("row")
    tile_rows = p_tiles.shape[0]
    cycle = tile_rows * n
    first_row = lax.axis_index("row") * tile_rows
    inv_p, idx_w = slot_maps(p_cols, p_count, first_row, cycle)
    inv_m, _ = slot_maps(m_cols, m_count, first_row, cycle)
    order = basis_atom.shape[0]
    span = (tile_rows + 2 * BAND) * 64
    wrapped = jnp.concatenate([basis_atom, basis_atom[:span]])
    start = (first_row * 64 - BAND * 64) % order
    atoms = lax.dynamic_slice_in_dim(wrapped, start, span)
    count = atom_slot.shape[0]
    cid = jnp.sum(jnp.where(atoms[:, None] == jnp.arange(count, dtype=jnp.int32)[None, :],
                            atom_slot[None, :], 0), axis=1, keepdims=True)
    smem = pl.BlockSpec(memory_space=pltpu.SMEM)
    vmem = pl.BlockSpec(memory_space=pltpu.VMEM)
    w, f = pl.pallas_call(
        functools.partial(kernel, n),
        out_shape=(jax.ShapeDtypeStruct((tile_rows, 64, 1024), F32),
                   jax.ShapeDtypeStruct((8, count), F32)),
        in_specs=[smem] * 3 + [vmem] * 4,
        out_specs=(vmem, vmem),
        scratch_shapes=[
            pltpu.VMEM((17, 256, 64), BF),
            pltpu.VMEM((17, 256, 64), BF),
            pltpu.VMEM((17, 256, 64), BF),
            pltpu.VMEM((256, 10 * L), BF),
            pltpu.VMEM((3, 256, 10 * L), BF),
            pltpu.VMEM((12 * L, 9 * L), BF),
            pltpu.VMEM((20 * L, 9 * L), BF),
            pltpu.VMEM((256, 18 * L), F32),
            pltpu.VMEM((256, 18 * L), BF),
            pltpu.VMEM((256, 10 * L), F32),
            pltpu.VMEM((21, 256, 64), F32),
            pltpu.VMEM((10 * L, count), BF),
            pltpu.SemaphoreType.DMA((4,)),
            pltpu.SemaphoreType.DMA((4,)),
            pltpu.SemaphoreType.DMA((8,)),
            pltpu.SemaphoreType.DMA((8,)),
        ],
        compiler_params=pltpu.CompilerParams(
            collective_id=0, has_side_effects=True, vmem_limit_bytes=56 * 1024 * 1024),
    )(inv_p, inv_m, idx_w, p_tiles, m_tiles, g_tiles, cid)
    forces = lax.psum_scatter(f[:3], "row", scatter_dimension=1, tiled=True)
    return w, forces


def solution(mesh):
    both = ("groups", "row")
    return jax.shard_map(
        body,
        mesh=mesh,
        in_specs=(P(both, None, None), P(both, None), P(both), P(both, None, None),
                  P(both, None), P(both), P(both, None, None, None), P("groups"), P("groups")),
        out_specs=(P(both, None, None), P(None, both)),
        check_vma=False,
    )
```

```python
import functools
import jax
import jax.numpy as jnp
from jax import lax
from jax.experimental import pallas as pl
from jax.experimental.pallas import tpu as pltpu
from jax.sharding import PartitionSpec as P

BAND = 8
L = 128
F32 = jnp.float32
BF = jnp.bfloat16
MESH = pl.DeviceIdType.MESH


def kernel(n, inverse, cols_p, count_p, p_ref, m_ref, g_ref, basis_ref, slot_ref, w_ref, f_ref,
           pt, mt, gt, pfull, gfull, mbuf, pbuf, xacc, xb, wacc, wt, onehot, fsend, frecv,
           ms, mr, ps, pr, fs, fr):
    me = lax.axis_index("row")
    core = lax.rem(me, 2)
    sibling = me + 1 - 2 * core

    def at(shift):
        return lax.rem(me + shift + n, n)

    side = 1 - 2 * lax.rem(lax.div(me, 2), 2)
    partner, onward, up2, dn2 = at(2 * side), at(4 * side), at(4), at(-4)
    barrier = pltpu.get_barrier_semaphore()

    def greet(i, carry):
        pl.semaphore_signal(barrier, inc=1, device_id={"row": at(i)}, device_id_type=MESH)
        return carry

    lax.fori_loop(1, n, greet, 0)

    def rows(at_super, count=2):
        return pl.ds(pl.multiple_of(at_super * L, L), count * L)

    def split(src, r, dst):
        for p in range(8):
            v = src[:, p * L:(p + 1) * L]
            dst[2 * p, r * 64:(r + 1) * 64, :] = v[:, :64]
            dst[2 * p + 1, r * 64:(r + 1) * 64, :] = v[:, 64:]
        dst[16, r * 64:(r + 1) * 64, :] = jnp.zeros((64, 64), BF)

    def pick(src, first, r, u):
        a = src[inverse[first + r, 2 * u], r * 64:(r + 1) * 64, :]
        b = src[inverse[first + r, 2 * u + 1], r * 64:(r + 1) * 64, :]
        return jnp.concatenate([a, b], axis=1)

    for r in range(4):
        split(m_ref.at[r], r, mt)
        sup = r // 2
        for u in range(sup, sup + 9):
            mbuf[pl.ds(pl.multiple_of((4 + 2 * core) * L, L) + r * 64, 64),
                 (u - sup) * L:(u - sup + 1) * L] = pick(mt, 4, r, u)
    pl.semaphore_wait(barrier, n - 1)

    def copy(buf, src_at, dst_at, col, width, sends, recvs, i, peer, count=2):
        cols = pl.ds(col, width * L)
        return pltpu.make_async_remote_copy(
            src_ref=buf.at[rows(src_at, count), cols], dst_ref=buf.at[rows(dst_at, count), cols],
            send_sem=sends.at[i], recv_sem=recvs.at[i],
            device_id={"row": peer}, device_id_type=MESH)

    own_m = 4 + 2 * core
    m_near, m_back = 4 + 4 * side + 2 * core, 4 - 4 * side + 2 * core
    m_par = [copy(mbuf, own_m + h, m_back + h, 0, 9, ms, mr, h, partner, 1) for h in range(2)]
    m_rel = [copy(mbuf, m_near + h, m_back + h, 0, 9, ms, mr, 2 + h, onward, 1) for h in range(2)]
    m_sib = copy(mbuf, own_m, own_m, 0, 9, ms, mr, 4, sibling)
    f_at = 8 - 6 * core
    m_fwd = copy(mbuf, f_at, f_at, 0, 9, ms, mr, 5, sibling)
    fwd_early = side == 1 - 2 * core
    m_par[0].start()
    m_par[1].start()
    m_sib.start()

    own_p = 8 + 2 * core
    for r in range(4):
        split(p_ref.at[r], r, pt)
        sup = r // 2
        for u in range(10):
            if sup <= u < sup + 9:
                v = pick(pt, 0, r, u)
                pfull[r * 64:(r + 1) * 64, u * L:(u + 1) * L] = v
                pbuf[pl.ds(pl.multiple_of(own_p * L, L) + r * 64, 64),
                     (u - sup) * L:(u - sup + 1) * L] = v
            else:
                pfull[r * 64:(r + 1) * 64, u * L:(u + 1) * L] = jnp.zeros((64, L), BF)
    p_near, p_back = 8 + 4 * side + 2 * core, 8 - 4 * side + 2 * core
    near_col = pl.multiple_of((1 - side) // 2 * L, L)
    back_col = pl.multiple_of((1 + side) // 2 * L, L)
    p_par = [copy(pbuf, own_p + h, p_back + h, 0, 9, ps, pr, h, partner, 1) for h in range(2)]
    p_rel = [copy(pbuf, p_near + h, p_back + h, back_col, 8, ps, pr, 2 + h, onward, 1)
             for h in range(2)]
    p_up2 = copy(pbuf, own_p, 2 * core, 5 * L, 4, ps, pr, 4, up2)
    p_dn2 = copy(pbuf, own_p, 16 + 2 * core, 0, 4, ps, pr, 5, dn2)
    p_sib = copy(pbuf, own_p, own_p, 0, 9, ps, pr, 6, sibling)
    p_fwd_a = copy(pbuf, p_near, p_near, near_col, 8, ps, pr, 7, sibling)
    p_fwd_b = copy(pbuf, p_back, p_back, back_col, 8, ps, pr, 8, sibling)
    far_at = 16 - 14 * core
    p_fwd_c = copy(pbuf, far_at, far_at, pl.multiple_of(core * 5 * L, L), 4, ps, pr, 9, sibling)
    for c in (*p_par, p_up2, p_dn2, p_sib):
        c.start()

    for c in range(3):
        for r in range(4):
            split(g_ref.at[r, c], r, gt)
            for u in range(10):
                gfull[c, r * 64:(r + 1) * 64, u * L:(u + 1) * L] = pick(gt, 0, r, u)
    slots = onehot.shape[0]
    lines = [basis_ref[pl.ds(lax.rem(2 * me - 4 + k + 2 * n, 2 * n), 1), :] for k in range(10)]
    atoms = jnp.concatenate(lines, axis=1)
    high_slot = slot_ref[...] // 64
    pair = jnp.concatenate([high_slot, slot_ref[...] - 64 * high_slot], axis=0).astype(F32)
    pair = jnp.concatenate([pair, jnp.zeros((6, slots), F32)], axis=0).astype(BF)

    def mark(values):
        for s in range(slots // L):
            ids = lax.broadcasted_iota(jnp.int32, (L, 10 * L), 0) + s * L
            onehot[s * L:(s + 1) * L, :] = jnp.where(values == ids, 1.0, 0.0).astype(BF)

    mark(atoms)
    found = jnp.dot(pair, onehot[...], preferred_element_type=F32)
    mark((64.0 * found[0:1] + found[1:2]).astype(jnp.int32))

    xacc[...] = jnp.zeros(xacc.shape, F32)
    wacc[...] = jnp.zeros(wacc.shape, F32)

    def add_x(j):
        xacc[:, j * L:(j + 9) * L] += jnp.dot(
            pfull[:, j * L:(j + 1) * L], mbuf[rows(j + 2 * core, 1), :],
            preferred_element_type=F32)

    def add_w(k):
        q0, q1 = max(0, 8 - k), min(8, 17 - k)
        m0 = k + q0 - 8
        width = q1 - q0 + 1
        wacc[:, m0 * L:(m0 + width) * L] += jnp.dot(
            xb[:, k * L:(k + 1) * L],
            pbuf[rows(k + 2 * core, 1), q0 * L:(q1 + 1) * L],
            preferred_element_type=F32)

    for h in range(2):
        m_par[h].wait_recv()
        m_rel[h].start()

    @pl.when(fwd_early)
    def _():
        m_fwd.start()

    add_x(4)
    add_x(5)
    for h in range(2):
        p_par[h].wait_recv()
        p_rel[h].start()
    p_fwd_a.start()
    p_up2.wait_recv()
    p_dn2.wait_recv()
    p_fwd_c.start()
    m_rel[0].wait_recv()
    m_rel[1].wait_recv()

    @pl.when(jnp.logical_not(fwd_early))
    def _():
        m_fwd.start()

    for j in (0, 1, 8, 9):
        add_x(j)
    m_sib.wait_recv()
    m_fwd.wait_recv()
    for j in (2, 3, 6, 7):
        add_x(j)
    xb[...] = xacc[...].astype(BF)
    for k in (8, 9, 0, 1, 16, 17):
        add_w(k)
    p_fwd_c.wait_recv()
    p_rel[0].wait_recv()
    p_rel[1].wait_recv()
    p_fwd_b.start()
    for k in (4, 5, 12, 13):
        add_w(k)
    p_sib.wait_recv()
    p_fwd_a.wait_recv()
    p_fwd_b.wait_recv()
    for k in (6, 7, 10, 11, 2, 3, 14, 15):
        add_w(k)

    lane = lax.broadcasted_iota(jnp.int32, (4 * 64, L), 1)
    by_row = jnp.zeros((4 * 64, L), F32)
    sub = lax.broadcasted_iota(jnp.int32, (8, 10 * L), 0)
    by_col = jnp.zeros((8, 10 * L), F32)
    for c in range(3):
        prod = wacc[...] * gfull[c].astype(F32)
        by_row = jnp.where(lane == c, jnp.sum(prod, axis=1, keepdims=True), by_row)
        by_col = jnp.where(sub == c, jnp.sum(prod, axis=0, keepdims=True), by_col)
    net_rows = jnp.transpose(by_row)[:8]
    net = jnp.concatenate(
        [-by_col[:, :4 * L], net_rows - by_col[:, 4 * L:6 * L], -by_col[:, 6 * L:]], axis=1)
    high = net.astype(BF).astype(F32)
    rest = net - high
    mid = rest.astype(BF).astype(F32)
    low = rest - mid
    parts = jnp.concatenate([high, mid, low, jnp.zeros_like(low)], axis=0).astype(BF)
    summed = lax.dot_general(parts, onehot[...], (((1,), (1,)), ((), ())),
                             preferred_element_type=F32)
    terms = -2.0 * (summed[0:8] + summed[8:16] + summed[16:24])
    share = slots // n
    for d in range(n):
        fsend[d, :, 0:share] = terms[:, d * share:(d + 1) * share]

    def force_copy(i):
        to = at(i)
        return pltpu.make_async_remote_copy(
            src_ref=fsend.at[to], dst_ref=frecv.at[i], send_sem=fs.at[i], recv_sem=fr.at[i],
            device_id={"row": to}, device_id_type=MESH)

    def force_start(i, carry):
        force_copy(i).start()
        return carry

    def force_wait(i, total):
        force_copy(i).wait_recv()
        return total + frecv[i]

    def force_done(i, carry):
        force_copy(i).wait_send()
        return carry

    lax.fori_loop(1, n, force_start, 0)

    for t in range(20):
        wt[t] = wacc[:, t * 64:(t + 1) * 64]
    wt[20] = jnp.zeros((4 * 64, 64), F32)

    def place(r, s):
        off = cols_p[r, s] - (4 * me + r) + BAND
        off = jnp.where(off < 0, off + 4 * n, off)
        off = jnp.where(off >= 4 * n, off - 4 * n, off)
        return jnp.where(s < count_p[r], off + r, 20)

    for r in range(4):
        for p in range(8):
            a = wt[place(r, 2 * p), r * 64:(r + 1) * 64, :]
            b = wt[place(r, 2 * p + 1), r * 64:(r + 1) * 64, :]
            w_ref[r, :, p * L:(p + 1) * L] = jnp.concatenate([a, b], axis=1)

    total = lax.fori_loop(1, n, force_wait, fsend[me])
    f_ref[...] = total[0:3, 0:share]
    lax.fori_loop(1, n, force_done, 0)
    for c in (*m_par, *m_rel, m_sib, m_fwd, *p_par, *p_rel, p_up2, p_dn2, p_sib,
              p_fwd_a, p_fwd_b, p_fwd_c):
        c.wait_send()


def slot_maps(cols, counts, first_row, cycle):
    lists, slot_count = cols.shape
    tile_rows = lists // 2
    local = (jnp.arange(lists, dtype=jnp.int32) % tile_rows)[:, None]
    place = (cols - (first_row + local) + BAND) % cycle + local
    slot = jnp.arange(slot_count, dtype=jnp.int32)[None, :]
    place = jnp.where(slot < counts[:, None], place, -1)
    hit = place[:, :, None] == jnp.arange(tile_rows + 2 * BAND, dtype=jnp.int32)
    return slot_count + jnp.sum(jnp.where(hit, slot[:, :, None] - slot_count, 0), axis=1)


def body(p_tiles, p_cols, p_count, m_tiles, m_cols, m_count, g_tiles, basis_atom, atom_slot):
    n = lax.axis_size("row")
    tile_rows = p_tiles.shape[0]
    first_row = lax.axis_index("row") * tile_rows
    inverse = slot_maps(jnp.concatenate([p_cols, m_cols]), jnp.concatenate([p_count, m_count]),
                        first_row, tile_rows * n)
    count = atom_slot.shape[0]
    smem = pl.BlockSpec(memory_space=pltpu.SMEM)
    vmem = pl.BlockSpec(memory_space=pltpu.VMEM)
    w, f = pl.pallas_call(
        functools.partial(kernel, n),
        out_shape=(jax.ShapeDtypeStruct((tile_rows, 64, 1024), F32),
                   jax.ShapeDtypeStruct((3, count // n), F32)),
        in_specs=[smem] * 3 + [vmem] * 5,
        out_specs=(vmem, vmem),
        scratch_shapes=[
            pltpu.VMEM((17, 256, 64), BF),
            pltpu.VMEM((17, 256, 64), BF),
            pltpu.VMEM((17, 256, 64), BF),
            pltpu.VMEM((256, 10 * L), BF),
            pltpu.VMEM((3, 256, 10 * L), BF),
            pltpu.VMEM((12 * L, 9 * L), BF),
            pltpu.VMEM((20 * L, 9 * L), BF),
            pltpu.VMEM((256, 18 * L), F32),
            pltpu.VMEM((256, 18 * L), BF),
            pltpu.VMEM((256, 10 * L), F32),
            pltpu.VMEM((21, 256, 64), F32),
            pltpu.VMEM((count, 10 * L), BF),
            pltpu.VMEM((n, 8, L), F32),
            pltpu.VMEM((n, 8, L), F32),
            pltpu.SemaphoreType.DMA((6,)),
            pltpu.SemaphoreType.DMA((6,)),
            pltpu.SemaphoreType.DMA((10,)),
            pltpu.SemaphoreType.DMA((10,)),
            pltpu.SemaphoreType.DMA((n,)),
            pltpu.SemaphoreType.DMA((n,)),
        ],
        compiler_params=pltpu.CompilerParams(
            collective_id=0, has_side_effects=True, vmem_limit_bytes=56 * 1024 * 1024),
    )(inverse, p_cols, p_count, p_tiles, m_tiles, g_tiles,
      basis_atom.reshape(-1, L), atom_slot.reshape(1, -1))
    return w, f


def solution(mesh):
    both = ("groups", "row")
    return jax.shard_map(
        body,
        mesh=mesh,
        in_specs=(P(both, None, None), P(both, None), P(both), P(both, None, None),
                  P(both, None), P(both), P(both, None, None, None), P("groups"), P("groups")),
        out_specs=(P(both, None, None), P(None, both)),
        check_vma=False,
    )
```

```python
import functools
import jax
import jax.numpy as jnp
from jax import lax
from jax.experimental import pallas as pl
from jax.experimental.pallas import tpu as pltpu
from jax.sharding import PartitionSpec as P

BAND = 8
L = 128
F32 = jnp.float32
BF = jnp.bfloat16
MESH = pl.DeviceIdType.MESH


def kernel(n, inverse, cols_p, count_p, p_ref, m_ref, g_ref, basis_ref, slot_ref, w_ref, f_ref,
           pt, mt, gt, pfull, gfull, mbuf, pbuf, xacc, xb, wacc, wt, onehot, fsend, frecv,
           ms, mr, ps, pr, fs, fr):
    me = lax.axis_index("row")
    core = lax.rem(me, 2)
    sibling = me + 1 - 2 * core

    def at(shift):
        return lax.rem(me + shift + n, n)

    side = 1 - 2 * lax.rem(lax.div(me, 2), 2)
    partner, onward, up2, dn2 = at(2 * side), at(4 * side), at(4), at(-4)
    barrier = pltpu.get_barrier_semaphore()

    def greet(i, carry):
        pl.semaphore_signal(barrier, inc=1, device_id={"row": at(i)}, device_id_type=MESH)
        return carry

    lax.fori_loop(1, n, greet, 0)

    def rows(at_super, count=2):
        return pl.ds(pl.multiple_of(at_super * L, L), count * L)

    def split(src, r, dst):
        for p in range(8):
            v = src[:, p * L:(p + 1) * L]
            dst[2 * p, r * 64:(r + 1) * 64, :] = v[:, :64]
            dst[2 * p + 1, r * 64:(r + 1) * 64, :] = v[:, 64:]
        dst[16, r * 64:(r + 1) * 64, :] = jnp.zeros((64, 64), BF)

    def pick(src, first, r, u):
        a = src[inverse[first + r, 2 * u], r * 64:(r + 1) * 64, :]
        b = src[inverse[first + r, 2 * u + 1], r * 64:(r + 1) * 64, :]
        return jnp.concatenate([a, b], axis=1)

    for r in range(4):
        split(m_ref.at[r], r, mt)
        sup = r // 2
        for u in range(sup, sup + 9):
            mbuf[pl.ds(pl.multiple_of((4 + 2 * core) * L, L) + r * 64, 64),
                 (u - sup) * L:(u - sup + 1) * L] = pick(mt, 4, r, u)
    pl.semaphore_wait(barrier, n - 1)

    def copy(buf, src_at, dst_at, col, width, sends, recvs, i, peer, count=2):
        cols = pl.ds(col, width * L)
        return pltpu.make_async_remote_copy(
            src_ref=buf.at[rows(src_at, count), cols], dst_ref=buf.at[rows(dst_at, count), cols],
            send_sem=sends.at[i], recv_sem=recvs.at[i],
            device_id={"row": peer}, device_id_type=MESH)

    own_m = 4 + 2 * core
    m_near, m_back = 4 + 4 * side + 2 * core, 4 - 4 * side + 2 * core
    m_par = [copy(mbuf, own_m + h, m_back + h, 0, 9, ms, mr, h, partner, 1) for h in range(2)]
    m_rel = [copy(mbuf, m_near + h, m_back + h, 0, 9, ms, mr, 2 + h, onward, 1) for h in range(2)]
    m_sib = copy(mbuf, own_m, own_m, 0, 9, ms, mr, 4, sibling)
    f_at = 8 - 6 * core
    m_fwd = copy(mbuf, f_at, f_at, 0, 9, ms, mr, 5, sibling)
    fwd_early = side == 1 - 2 * core
    m_par[0].start()
    m_par[1].start()
    m_sib.start()

    own_p = 8 + 2 * core
    for r in range(4):
        split(p_ref.at[r], r, pt)
        sup = r // 2
        for u in range(10):
            if sup <= u < sup + 9:
                v = pick(pt, 0, r, u)
                pfull[r * 64:(r + 1) * 64, u * L:(u + 1) * L] = v
                pbuf[pl.ds(pl.multiple_of(own_p * L, L) + r * 64, 64),
                     (u - sup) * L:(u - sup + 1) * L] = v
            else:
                pfull[r * 64:(r + 1) * 64, u * L:(u + 1) * L] = jnp.zeros((64, L), BF)
    p_near, p_back = 8 + 4 * side + 2 * core, 8 - 4 * side + 2 * core
    near_col = pl.multiple_of((1 - side) // 2 * L, L)
    back_col = pl.multiple_of((1 + side) // 2 * L, L)
    p_par = [copy(pbuf, own_p + h, p_back + h, 0, 9, ps, pr, h, partner, 1) for h in range(2)]
    def in_case(act):
        for way in (1, -1):
            for b in range(2):
                @pl.when(jnp.logical_and(side == way, core == b))
                def _(way=way, b=b):
                    act(way, b)

    def back_cols(way, b, h):
        return (4 - 2 * b - h, 5 + 2 * b + h) if way == 1 else (0, 8 - 2 * b - h)

    def p_rel(way, b, h):
        col, width = back_cols(way, b, h)
        return copy(pbuf, p_near + h, p_back + h, col * L, width, ps, pr, 2 + h, onward, 1)

    def p_fwd_b(way, b, h):
        col, width = back_cols(way, b, h)
        return copy(pbuf, p_back + h, p_back + h, col * L, width, ps, pr, 8 + h, sibling, 1)

    def from_sib(way, b, h):
        col, width = back_cols(way, 1 - b, h)
        return copy(pbuf, p_back + h, p_back + h, col * L, width, ps, pr, 8 + h, sibling, 1)

    def p_up2(b):
        return copy(pbuf, own_p, 2 * core, (7 - 2 * b) * L, 2 + 2 * b, ps, pr, 4, up2)

    def p_dn2(b):
        return copy(pbuf, own_p, 16 + 2 * core, 0, 4 - 2 * b, ps, pr, 5, dn2)

    p_sib = copy(pbuf, own_p, own_p, 0, 9, ps, pr, 6, sibling)
    p_fwd_a = copy(pbuf, p_near, p_near, near_col, 8, ps, pr, 7, sibling)
    far_at = 16 - 14 * core
    p_fwd_c = copy(pbuf, far_at, far_at, pl.multiple_of(core * 5 * L, L), 4, ps, pr, 10, sibling)
    def start_far(way, b):
        p_up2(b).start()
        p_dn2(b).start()

    p_par[0].start()
    p_par[1].start()
    in_case(start_far)
    p_sib.start()

    xacc[...] = jnp.zeros(xacc.shape, F32)
    wacc[...] = jnp.zeros(wacc.shape, F32)

    def add_x(j):
        xacc[:, j * L:(j + 9) * L] += jnp.dot(
            pfull[:, j * L:(j + 1) * L], mbuf[rows(j + 2 * core, 1), :],
            preferred_element_type=F32)

    def add_w(k):
        q0, q1 = max(0, 8 - k), min(8, 17 - k)
        m0 = k + q0 - 8
        width = q1 - q0 + 1
        wacc[:, m0 * L:(m0 + width) * L] += jnp.dot(
            xb[:, k * L:(k + 1) * L],
            pbuf[rows(k + 2 * core, 1), q0 * L:(q1 + 1) * L],
            preferred_element_type=F32)

    for h in range(2):
        m_par[h].wait_recv()
        m_rel[h].start()

    @pl.when(fwd_early)
    def _():
        m_fwd.start()

    add_x(4)
    add_x(5)

    for c in range(3):
        for r in range(4):
            split(g_ref.at[r, c], r, gt)
            for u in range(10):
                gfull[c, r * 64:(r + 1) * 64, u * L:(u + 1) * L] = pick(gt, 0, r, u)
    slots = onehot.shape[0]
    lines = [basis_ref[pl.ds(lax.rem(2 * me - 4 + k + 2 * n, 2 * n), 1), :] for k in range(10)]
    atoms = jnp.concatenate(lines, axis=1)
    slot_row = jnp.concatenate([slot_ref[k:k + 1, :] for k in range(slots // L)], axis=1)
    high_slot = slot_row // 64
    pair = jnp.concatenate([high_slot, slot_row - 64 * high_slot], axis=0).astype(F32)
    pair = jnp.concatenate([pair, jnp.zeros((6, slots), F32)], axis=0).astype(BF)

    def mark(values):
        for s in range(slots // L):
            ids = lax.broadcasted_iota(jnp.int32, (L, 10 * L), 0) + s * L
            onehot[s * L:(s + 1) * L, :] = jnp.where(values == ids, 1.0, 0.0).astype(BF)

    mark(atoms)
    found = jnp.dot(pair, onehot[...], preferred_element_type=F32)
    mark((64.0 * found[0:1] + found[1:2]).astype(jnp.int32))

    for h in range(2):
        p_par[h].wait_recv()
        in_case(lambda way, b, h=h: p_rel(way, b, h).start())
    p_fwd_a.start()

    def wait_far(way, b):
        p_up2(b).wait_recv()
        p_dn2(b).wait_recv()

    in_case(wait_far)
    p_fwd_c.start()
    m_rel[0].wait_recv()
    m_rel[1].wait_recv()

    @pl.when(jnp.logical_not(fwd_early))
    def _():
        m_fwd.start()

    for j in (0, 1, 8, 9):
        add_x(j)
    m_sib.wait_recv()
    m_fwd.wait_recv()
    for j in (2, 3, 6, 7):
        add_x(j)
    xb[...] = xacc[...].astype(BF)
    p_fwd_c.wait_recv()
    p_sib.wait_recv()
    p_fwd_a.wait_recv()

    def back_rows(way, b):
        first = 8 - 4 * way
        other = first + 2 - 4 * b
        return (first, first + 1), (other, other + 1)

    def early(way, b):
        direct, handed = back_rows(way, b)
        for k in range(18):
            if k not in direct + handed:
                add_w(k)

    def late(way, b):
        direct, handed = back_rows(way, b)
        for h in range(2):
            p_rel(way, b, h).wait_recv()
            p_fwd_b(way, b, h).start()
        for k in direct:
            add_w(k)
        for h in range(2):
            from_sib(way, b, h).wait_recv()
            add_w(handed[h])

    in_case(early)
    in_case(late)

    lane = lax.broadcasted_iota(jnp.int32, (4 * 64, L), 1)
    by_row = jnp.zeros((4 * 64, L), F32)
    sub = lax.broadcasted_iota(jnp.int32, (8, 10 * L), 0)
    by_col = jnp.zeros((8, 10 * L), F32)
    for c in range(3):
        prod = wacc[...] * gfull[c].astype(F32)
        by_row = jnp.where(lane == c, jnp.sum(prod, axis=1, keepdims=True), by_row)
        by_col = jnp.where(sub == c, jnp.sum(prod, axis=0, keepdims=True), by_col)
    net_rows = jnp.transpose(by_row)[:8]
    net = jnp.concatenate(
        [-by_col[:, :4 * L], net_rows - by_col[:, 4 * L:6 * L], -by_col[:, 6 * L:]], axis=1)
    high = net.astype(BF).astype(F32)
    rest = net - high
    mid = rest.astype(BF).astype(F32)
    low = rest - mid
    parts = jnp.concatenate([high, mid, low, jnp.zeros_like(low)], axis=0).astype(BF)
    summed = lax.dot_general(parts, onehot[...], (((1,), (1,)), ((), ())),
                             preferred_element_type=F32)
    terms = -2.0 * (summed[0:8] + summed[8:16] + summed[16:24])
    share = slots // n
    for d in range(n):
        fsend[d, :, 0:share] = terms[:, d * share:(d + 1) * share]

    def force_copy(i):
        to = at(i)
        return pltpu.make_async_remote_copy(
            src_ref=fsend.at[to], dst_ref=frecv.at[i], send_sem=fs.at[i], recv_sem=fr.at[i],
            device_id={"row": to}, device_id_type=MESH)

    def force_start(i, carry):
        force_copy(i).start()
        return carry

    def force_wait(i, total):
        force_copy(i).wait_recv()
        return total + frecv[i]

    def force_done(i, carry):
        force_copy(i).wait_send()
        return carry

    lax.fori_loop(1, n, force_start, 0)

    for t in range(20):
        wt[t] = wacc[:, t * 64:(t + 1) * 64]
    wt[20] = jnp.zeros((4 * 64, 64), F32)

    def place(r, s):
        off = cols_p[r, s] - (4 * me + r) + BAND
        off = jnp.where(off < 0, off + 4 * n, off)
        off = jnp.where(off >= 4 * n, off - 4 * n, off)
        return jnp.where(s < count_p[r], off + r, 20)

    for r in range(4):
        for p in range(8):
            a = wt[place(r, 2 * p), r * 64:(r + 1) * 64, :]
            b = wt[place(r, 2 * p + 1), r * 64:(r + 1) * 64, :]
            w_ref[r, :, p * L:(p + 1) * L] = jnp.concatenate([a, b], axis=1)

    total = lax.fori_loop(1, n, force_wait, fsend[me])
    f_ref[...] = total[0:3, 0:share]
    lax.fori_loop(1, n, force_done, 0)
    for c in (*m_par, *m_rel, m_sib, m_fwd, *p_par, p_sib, p_fwd_a, p_fwd_c):
        c.wait_send()

    def sent(way, b):
        p_up2(b).wait_send()
        p_dn2(b).wait_send()
        for h in range(2):
            p_rel(way, b, h).wait_send()
            p_fwd_b(way, b, h).wait_send()

    in_case(sent)


def slot_maps(cols, counts, first_row, cycle):
    lists, slot_count = cols.shape
    tile_rows = lists // 2
    local = (jnp.arange(lists, dtype=jnp.int32) % tile_rows)[:, None]
    place = (cols - (first_row + local) + BAND) % cycle + local
    slot = jnp.arange(slot_count, dtype=jnp.int32)[None, :]
    place = jnp.where(slot < counts[:, None], place, -1)
    hit = place[:, :, None] == jnp.arange(tile_rows + 2 * BAND, dtype=jnp.int32)
    return slot_count + jnp.sum(jnp.where(hit, slot[:, :, None] - slot_count, 0), axis=1)


def body(p_tiles, p_cols, p_count, m_tiles, m_cols, m_count, g_tiles, basis_atom, atom_slot):
    n = lax.axis_size("row")
    tile_rows = p_tiles.shape[0]
    first_row = lax.axis_index("row") * tile_rows
    inverse = slot_maps(jnp.concatenate([p_cols, m_cols]), jnp.concatenate([p_count, m_count]),
                        first_row, tile_rows * n)
    count = atom_slot.shape[0]
    smem = pl.BlockSpec(memory_space=pltpu.SMEM)
    vmem = pl.BlockSpec(memory_space=pltpu.VMEM)
    w, f = pl.pallas_call(
        functools.partial(kernel, n),
        out_shape=(jax.ShapeDtypeStruct((tile_rows, 64, 1024), F32),
                   jax.ShapeDtypeStruct((3, count // n), F32)),
        in_specs=[smem] * 3 + [vmem] * 5,
        out_specs=(vmem, vmem),
        scratch_shapes=[
            pltpu.VMEM((17, 256, 64), BF),
            pltpu.VMEM((17, 256, 64), BF),
            pltpu.VMEM((17, 256, 64), BF),
            pltpu.VMEM((256, 10 * L), BF),
            pltpu.VMEM((3, 256, 10 * L), BF),
            pltpu.VMEM((12 * L, 9 * L), BF),
            pltpu.VMEM((20 * L, 9 * L), BF),
            pltpu.VMEM((256, 18 * L), F32),
            pltpu.VMEM((256, 18 * L), BF),
            pltpu.VMEM((256, 10 * L), F32),
            pltpu.VMEM((21, 256, 64), F32),
            pltpu.VMEM((count, 10 * L), BF),
            pltpu.VMEM((n, 8, L), F32),
            pltpu.VMEM((n, 8, L), F32),
            pltpu.SemaphoreType.DMA((6,)),
            pltpu.SemaphoreType.DMA((6,)),
            pltpu.SemaphoreType.DMA((11,)),
            pltpu.SemaphoreType.DMA((11,)),
            pltpu.SemaphoreType.DMA((n,)),
            pltpu.SemaphoreType.DMA((n,)),
        ],
        compiler_params=pltpu.CompilerParams(
            collective_id=0, has_side_effects=True, vmem_limit_bytes=56 * 1024 * 1024),
    )(inverse, p_cols, p_count, p_tiles, m_tiles, g_tiles,
      basis_atom.reshape(-1, L), atom_slot.reshape(-1, L))
    return w, f


def solution(mesh):
    both = ("groups", "row")
    return jax.shard_map(
        body,
        mesh=mesh,
        in_specs=(P(both, None, None), P(both, None), P(both), P(both, None, None),
                  P(both, None), P(both), P(both, None, None, None), P("groups"), P("groups")),
        out_specs=(P(both, None, None), P(None, both)),
        check_vma=False,
    )
```
